32 devices in a mesh: expert: 4 (over z), dp: 8 (over y, x, core).
Axes of the slice: x: 2, y: 2, z: 4, core: 2. Of those that a mesh axis runs over, the one named last changes fastest.
Arguments:
- gradient: float32 [4, 8, 512, 1024], P('expert', 'dp'), may hold values from -200 to 200
- first_moment: float32 [4, 512, 1024], P('expert', 'dp'), may hold values from -0.6 to 0.6
- second_moment: float32 [4, 512, 1024], P('expert', 'dp'), may hold values from 0.002 to 0.02
- left_basis: float32 [4, 512, 512], P('expert'), may hold values from -1 to 1
- right_basis: float32 [4, 2, 512, 512], P('expert'), may hold values from -1 to 1
Outputs:
- update: float32 [4, 512, 1024], P('expert')
- new_first: float32 [4, 512, 1024], P('expert', 'dp')
- new_second: float32 [4, 512, 1024], P('expert', 'dp')
The draws below stay inside these ranges and needn't reach their ends.
All inputs are finite; a program needn't handle non-finite values.
Results may differ from the reference program's by a relative error of at most 0.000092.
Values sent between devices are 32-bit elements; how exact they have to be, the bound alone decides.
A program may use at most 64 MiB of HBM per device.

```python
import math
import jax
import jax.numpy as jnp
from jax import lax

BLOCK = 512
RIGHT_BLOCKS = 2
COLS = 1024
EXPERTS = 4
REPLICAS = 8


def orthogonal(key, count):
    raw = jax.random.normal(key, (count, BLOCK, BLOCK), jnp.float32)
    basis, upper = jnp.linalg.qr(raw)
    return basis


def draw_gradient(key, part):
    noise_key, row_key, col_key = jax.random.split(jax.random.fold_in(key, 11), 3)
    row_scale = jnp.exp(jax.random.uniform(row_key, (EXPERTS, 1, BLOCK, 1), jnp.float32, jnp.log(0.5), jnp.log(5.0)))
    col_scale = jnp.exp(jax.random.uniform(col_key, (EXPERTS, 1, 1, COLS), jnp.float32, jnp.log(0.5), jnp.log(5.0)))
    noise = jnp.clip(jax.random.normal(noise_key, (EXPERTS, REPLICAS, BLOCK, COLS), jnp.float32), -6.0, 6.0)
    return noise * row_scale * col_scale


def draw_first_moment(key, part):
    noise_key, row_key = jax.random.split(jax.random.fold_in(key, 23), 2)
    rows = jnp.arange(BLOCK, dtype=jnp.float32) / (BLOCK - 1)
    experts = jnp.arange(EXPERTS, dtype=jnp.float32) / max(EXPERTS - 1, 1)
    ramp = jnp.exp(jnp.log(3.0) * (rows[None, :, None] + experts[:, None, None]) * 0.5)
    noise = jnp.clip(jax.random.normal(noise_key, (EXPERTS, BLOCK, COLS), jnp.float32), -3.0, 3.0)
    jitter = jax.random.uniform(row_key, (EXPERTS, BLOCK, 1), jnp.float32, 0.7, 1.3)
    return 0.05 * noise * ramp * jitter


def draw_left_basis(key, part):
    return orthogonal(jax.random.fold_in(key, 37), EXPERTS)


def draw_right_basis(key, part):
    basis = orthogonal(jax.random.fold_in(key, 41), EXPERTS * RIGHT_BLOCKS)
    return basis.reshape(EXPERTS, RIGHT_BLOCKS, BLOCK, BLOCK)


def level_of(own_key, dims, cuts, smallest, high):
    loudness, own = 1.0, jax.random.fold_in(own_key, 6)
    for position, blocks in cuts:
        steps = jnp.exp(jax.random.uniform(jax.random.fold_in(own, position), (blocks,), jnp.float32, smallest / len(cuts), high / len(cuts)))
        loudness = loudness * jnp.repeat(steps, dims[position] // blocks).reshape([-1 if axis == position else 1 for axis in range(len(dims))])
    return loudness


def setup_inputs(seed: int = 0) -> dict:
    keys = jax.random.split(jax.random.key(seed), 6)
    return {
        "gradient": draw_gradient(jax.random.fold_in(keys[5], 71), 0),
        "first_moment": draw_first_moment(jax.random.fold_in(keys[5], 71), 0),
        "second_moment": jnp.clip(jnp.exp(math.log(0.02) - 2.30258502 * jax.random.uniform(keys[2], (EXPERTS, BLOCK, COLS), jnp.float32) ** level_of(keys[2], (EXPERTS, BLOCK, COLS), ((0, 4), (1, 8)), -0.2, 0.2)), 0.002, 0.02),
        "left_basis": draw_left_basis(jax.random.fold_in(keys[5], 71), 0),
        "right_basis": draw_right_basis(jax.random.fold_in(keys[5], 71), 0),
    }


highest = lax.Precision.HIGHEST

def right_turn(x, basis):
    parts = x.reshape(x.shape[0], x.shape[1], RIGHT_BLOCKS, BLOCK)
    out = jnp.einsum('erbc,ebcd->erbd', parts, basis, precision=highest)
    return out.reshape(x.shape)

def right_back(x, basis):
    parts = x.reshape(x.shape[0], x.shape[1], RIGHT_BLOCKS, BLOCK)
    out = jnp.einsum('erbd,ebcd->erbc', parts, basis, precision=highest)
    return out.reshape(x.shape)

def reference(gradient, first_moment, second_moment, left_basis, right_basis):
    summed = lax.optimization_barrier(jnp.sum(gradient, axis=1))
    left = jnp.einsum('ekr,ekc->erc', left_basis, summed, precision=highest)
    mean = right_turn(left, right_basis) / REPLICAS
    new_first = 0.9 * first_moment + 0.1 * mean
    new_second = 0.95 * second_moment + 0.05 * mean * mean
    normal = new_first / (jnp.sqrt(new_second) + 1e-08)
    scale = jnp.sqrt(jnp.sum(normal * normal) / (EXPERTS * BLOCK * COLS) + 1e-06)
    turned = right_back(normal, right_basis)
    back = jnp.einsum('ekr,erc->ekc', left_basis, turned, precision=highest)
    return (back / scale, new_first, new_second)
```

```python
import functools

import jax
import jax.numpy as jnp
from jax import lax
from jax.experimental import pallas as pl
from jax.experimental.pallas import tpu as pltpu
from jax.sharding import PartitionSpec as P

MESH = pl.DeviceIdType.MESH
NN = (((1,), (0,)), ((), ()))
NT = (((1,), (1,)), ((), ()))


def split(x):
    hi = x.astype(jnp.bfloat16)
    lo = (x - hi.astype(jnp.float32)).astype(jnp.bfloat16)
    return hi, lo


def dot3(a, b, dims=NN):
    dot = functools.partial(
        lax.dot_general, dimension_numbers=dims, preferred_element_type=jnp.float32
    )
    return dot(a[0], b[0]) + (dot(a[0], b[1]) + dot(a[1], b[0]))


def kernel(
    cfg, grad, first, second, left, right,
    back_out, scale_out, first_out, second_out,
    g, lf, rt, fm, sm, lt, gh, gl, lh, ll, ah, al, rh, rl,
    s1, r1, s2, r2, t, acc, zs, ds, sc,
    in_sem, g_sem, out_sem, b_sem, s1_s, s1_r, s2_s, s2_r, ag_s, ag_r, fw_s, fw_r, z_s, z_r, d_s, d_r,
):
    experts, n, chunk, count = cfg
    order, width = grad.shape
    blocks, depth = right.shape[0], right.shape[1]
    chips, rows = n // 2, order // n
    chunks, per = width // chunk, depth // chunk
    e, d = lax.axis_index("expert"), lax.axis_index("dp")
    chip, core = d // 2, d % 2
    sibling = chip * 2 + (1 - core)

    def other(k):
        return lax.rem(chip + k, chips) * 2 + core

    def source(k):
        return lax.rem(chip + chips - k, chips) * 2 + core

    def remote(src, dst, send, recv, to):
        return pltpu.make_async_remote_copy(
            src_ref=src, dst_ref=dst, send_sem=send, recv_sem=recv, device_id=to, device_id_type=MESH
        )

    barrier = pltpu.get_barrier_semaphore()
    for k in range(1, n):
        pl.semaphore_signal(barrier, inc=1, device_id=(e, lax.rem(d + k, n)), device_id_type=MESH)
    for k in range(1, experts):
        pl.semaphore_signal(barrier, inc=1, device_id=(lax.rem(e + k, experts), d), device_id_type=MESH)

    loads = [
        pltpu.make_async_copy(a, b, in_sem.at[i])
        for i, (a, b) in enumerate(((left, lf), (right, rt), (first, fm), (second, sm)))
    ]
    grads = [
        pltpu.make_async_copy(
            grad.at[:, pl.ds(q * chunk, chunk)], g.at[:, pl.ds(q * chunk, chunk)], g_sem.at[q]
        )
        for q in range(chunks)
    ]
    loads[0].start()
    for c in grads:
        c.start()
    for c in loads[1:]:
        c.start()

    loads[0].wait()
    lt[...] = jnp.transpose(lf[...]).reshape(n, rows, order)
    for side, parity in ((0, 1 - core), (1, core)):
        picked = jnp.concatenate([lt[2 * c + parity] for c in range(chips)], axis=0)
        ah[side], al[side] = split(picked)

    pl.semaphore_wait(barrier, n - 1 + experts - 1)

    sends = []
    firsts = []
    for q in range(chunks):
        cols = pl.ds(q * chunk, chunk)
        grads[q].wait()
        hi, lo = split(g[:, cols])
        gh[:, cols], gl[:, cols] = hi, lo
        s1[q] = dot3((ah[0], al[0]), (hi, lo))
        c = remote(s1.at[q], r1.at[q], s1_s.at[q], s1_r.at[q], (e, sibling))
        c.start()
        firsts.append(c)
    seconds = {}
    for q in range(chunks):
        cols = pl.ds(q * chunk, chunk)
        own = dot3((ah[1], al[1]), (gh[:, cols], gl[:, cols]))
        firsts[q].wait_recv()
        total = own + r1[q]
        for c in range(chips):
            s2[c, q] = total[c * rows : (c + 1) * rows]
        for k in range(1, chips):
            c = remote(
                s2.at[lax.rem(chip + k, chips), q], r2.at[k, q], s2_s.at[k, q], s2_r.at[k, q], (e, other(k))
            )
            c.start()
            seconds[k, q] = c
            sends.append(c)
    lh[...], ll[...] = split(lf[...])
    for c in loads[1:]:
        c.wait()
    for b in range(blocks):
        rh[b], rl[b] = split(rt[b])

    gathers = {}
    forwards = {}
    squares = jnp.zeros((1, 1), jnp.float32)
    for b in range(blocks):
        parts = []
        for q in range(b * per, (b + 1) * per):
            x = s2[chip, q]
            for k in range(1, chips):
                seconds[k, q].wait_recv()
                x = x + r2[k, q]
            parts.append(x)
        x = jnp.concatenate(parts, axis=1)
        cols = pl.ds(b * depth, depth)
        turn = (rh[b], rl[b])
        mean = dot3(split(x), turn) / n
        new_first = 0.9 * fm[:, cols] + 0.1 * mean
        new_second = 0.95 * sm[:, cols] + 0.05 * mean * mean
        normal = new_first / (jnp.sqrt(new_second) + 1e-08)
        t[b, d] = dot3(split(normal), turn, NT)
        for k in range(1, chips):
            c = remote(t.at[b, d], t.at[b, d], ag_s.at[b, k], ag_r.at[b, k], (e, other(k)))
            c.start()
            gathers[b, k] = c
            sends.append(c)
        c = remote(t.at[b, d], t.at[b, d], fw_s.at[b, 0], fw_r.at[b, 0], (e, sibling))
        c.start()
        forwards[b, 0] = c
        fm[:, cols] = new_first
        sm[:, cols] = new_second
        squares = squares + jnp.sum(
            jnp.sum(normal * normal, axis=0, keepdims=True), axis=1, keepdims=True
        )

    outs = [
        pltpu.make_async_copy(fm, first_out, out_sem.at[0]),
        pltpu.make_async_copy(sm, second_out, out_sem.at[1]),
    ]
    for c in outs:
        c.start()
    zs[e] = jnp.broadcast_to(squares, zs.shape[1:])
    tops = []
    for k in range(1, experts):
        c = remote(zs.at[e], zs.at[e], z_s.at[k], z_r.at[k], (lax.rem(e + k, experts), d))
        c.start()
        tops.append(c)

    for b in range(blocks):
        for k in range(1, chips):
            gathers[b, k].wait_recv()
            piece = t.at[b, source(k)]
            c = remote(piece, piece, fw_s.at[b, k], fw_r.at[b, k], (e, sibling))
            c.start()
            forwards[b, k] = c
        if b == 0:
            for c in tops:
                c.wait_recv()
            ds[d] = jnp.sum(zs[...], axis=0)
            peers = []
            for k in range(1, n):
                c = remote(ds.at[d], ds.at[d], d_s.at[k], d_r.at[k], (e, lax.rem(d + k, n)))
                c.start()
                peers.append(c)
        for k in range(chips):
            forwards[b, k].wait_recv()
        for j in range(per):
            cols = pl.ds(b * depth + j * chunk, chunk)
            piece = t[b, :, :, j * chunk : (j + 1) * chunk].reshape(order, chunk)
            acc[:, cols] = dot3((lh[...], ll[...]), split(piece))
        cols = pl.ds(b * depth, depth)
        c = pltpu.make_async_copy(acc.at[:, cols], back_out.at[:, cols], b_sem.at[b])
        c.start()
        outs.append(c)

    for c in peers:
        c.wait_recv()
    sc[...] = jnp.sqrt(jnp.sum(ds[...], axis=0) / count + 1e-06)
    c = pltpu.make_async_copy(sc, scale_out, out_sem.at[2])
    c.start()
    outs.append(c)
    for c in firsts + sends + list(forwards.values()) + tops + peers:
        c.wait_send()
    for c in outs:
        c.wait()


def per_device(gradient, first_moment, second_moment, left_basis, right_basis):
    held, _, order, width = gradient.shape
    blocks, depth = right_basis.shape[1], right_basis.shape[2]
    experts, n = lax.axis_size("expert"), lax.axis_size("dp")
    rows, chips = order // n, n // 2
    chunk = min(256, depth)
    chunks = width // chunk
    half = order // 2
    f32, bf16 = jnp.float32, jnp.bfloat16
    dma = pltpu.SemaphoreType.DMA
    tile = (8, 128)
    scratch = [
        pltpu.VMEM((order, width), f32),
        pltpu.VMEM((order, order), f32),
        pltpu.VMEM((blocks, depth, depth), f32),
        pltpu.VMEM((rows, width), f32),
        pltpu.VMEM((rows, width), f32),
        pltpu.VMEM((n, rows, order), f32),
        pltpu.VMEM((order, width), bf16),
        pltpu.VMEM((order, width), bf16),
        pltpu.VMEM((order, order), bf16),
        pltpu.VMEM((order, order), bf16),
        pltpu.VMEM((2, half, order), bf16),
        pltpu.VMEM((2, half, order), bf16),
        pltpu.VMEM((blocks, depth, depth), bf16),
        pltpu.VMEM((blocks, depth, depth), bf16),
        pltpu.VMEM((chunks, half, chunk), f32),
        pltpu.VMEM((chunks, half, chunk), f32),
        pltpu.VMEM((chips, chunks, rows, chunk), f32),
        pltpu.VMEM((chips, chunks, rows, chunk), f32),
        pltpu.VMEM((blocks, n, rows, depth), f32),
        pltpu.VMEM((order, width), f32),
        pltpu.VMEM((experts,) + tile, f32),
        pltpu.VMEM((n,) + tile, f32),
        pltpu.VMEM(tile, f32),
        dma((4,)), dma((chunks,)), dma((3,)), dma((blocks,)),
        dma((chunks,)), dma((chunks,)),
        dma((chips, chunks)), dma((chips, chunks)),
        dma((blocks, chips)), dma((blocks, chips)),
        dma((blocks, chips)), dma((blocks, chips)),
        dma((experts,)), dma((experts,)),
        dma((n,)), dma((n,)),
    ]
    cfg = (experts, n, chunk, held * experts * order * width)
    anywhere = pl.BlockSpec(memory_space=pl.ANY)
    back, scale, new_first, new_second = pl.pallas_call(
        functools.partial(kernel, cfg),
        out_shape=(
            jax.ShapeDtypeStruct((order, width), f32),
            jax.ShapeDtypeStruct(tile, f32),
            jax.ShapeDtypeStruct((rows, width), f32),
            jax.ShapeDtypeStruct((rows, width), f32),
        ),
        in_specs=[anywhere] * 5,
        out_specs=(anywhere,) * 4,
        scratch_shapes=scratch,
        compiler_params=pltpu.CompilerParams(
            collective_id=0, has_side_effects=True, vmem_limit_bytes=48 * 1024 * 1024
        ),
    )(
        gradient.reshape(order, width),
        first_moment.reshape(rows, width),
        second_moment.reshape(rows, width),
        left_basis.reshape(order, order),
        right_basis.reshape(blocks, depth, depth),
    )
    return (back / scale[0, 0])[None], new_first[None], new_second[None]


def solution(mesh):
    in_specs = (
        P("expert", "dp", None, None),
        P("expert", "dp", None),
        P("expert", "dp", None),
        P("expert", None, None),
        P("expert", None, None, None),
    )
    out_specs = (P("expert", None, None), P("expert", "dp", None), P("expert", "dp", None))
    return jax.shard_map(
        per_device, mesh=mesh, in_specs=in_specs, out_specs=out_specs, check_vma=False
    )
```

```python
import functools

import jax
import jax.numpy as jnp
from jax import lax
from jax.experimental import pallas as pl
from jax.experimental.pallas import tpu as pltpu
from jax.sharding import PartitionSpec as P

MESH = pl.DeviceIdType.MESH
NN = (((1,), (0,)), ((), ()))
NT = (((1,), (1,)), ((), ()))


def split(x):
    hi = x.astype(jnp.bfloat16)
    lo = (x - hi.astype(jnp.float32)).astype(jnp.bfloat16)
    return hi, lo


def dot3(a, b, dims=NN):
    dot = functools.partial(
        lax.dot_general, dimension_numbers=dims, preferred_element_type=jnp.float32
    )
    return dot(a[0], b[0]) + (dot(a[0], b[1]) + dot(a[1], b[0]))


def kernel(
    cfg, grad, first, second, left, right,
    back_out, scale_out, first_out, second_out,
    g, lf, rt, fm, sm, lt, gh, gl, lh, ll, ah, al, rh, rl,
    s1, r1, s2, r2, t, acc, zs, ds, sc,
    in_sem, g_sem, out_sem, b_sem, s1_s, s1_r, s2_s, s2_r, ag_s, ag_r, fw_s, fw_r, z_s, z_r, d_s, d_r,
):
    experts, n, chunk, count = cfg
    order, width = grad.shape
    blocks, depth = right.shape[0], right.shape[1]
    chips, rows = n // 2, order // n
    chunks, per = width // chunk, depth // chunk
    e, d = lax.axis_index("expert"), lax.axis_index("dp")
    chip, core = d // 2, d % 2
    sibling = chip * 2 + (1 - core)

    near = {k: lax.rem(chip + k, chips) for k in range(1, chips)}
    source = {k: lax.rem(chip + chips - k, chips) for k in range(1, chips)}

    def at(c):
        return (e, c * 2 + core)

    def remote(src, dst, send, recv, to):
        return pltpu.make_async_remote_copy(
            src_ref=src, dst_ref=dst, send_sem=send, recv_sem=recv, device_id=to, device_id_type=MESH
        )

    barrier = pltpu.get_barrier_semaphore()
    for k in range(1, n):
        pl.semaphore_signal(barrier, inc=1, device_id=(e, lax.rem(d + k, n)), device_id_type=MESH)
    for k in range(1, experts):
        pl.semaphore_signal(barrier, inc=1, device_id=(lax.rem(e + k, experts), d), device_id_type=MESH)

    loads = [
        pltpu.make_async_copy(a, b, in_sem.at[i])
        for i, (a, b) in enumerate(((left, lf), (right, rt), (first, fm), (second, sm)))
    ]
    grads = [
        pltpu.make_async_copy(
            grad.at[:, pl.ds(q * chunk, chunk)], g.at[:, pl.ds(q * chunk, chunk)], g_sem.at[q]
        )
        for q in range(chunks)
    ]
    loads[0].start()
    for c in grads:
        c.start()
    for c in loads[1:]:
        c.start()

    loads[0].wait()
    lt[...] = jnp.transpose(lf[...]).reshape(n, rows, order)
    for side, parity in ((0, 1 - core), (1, core)):
        picked = jnp.concatenate([lt[2 * c + parity] for c in range(chips)], axis=0)
        ah[side], al[side] = split(picked)

    pl.semaphore_wait(barrier, n - 1 + experts - 1)

    sends = []
    firsts = []
    seconds = {}

    def for_sibling(q):
        cols = pl.ds(q * chunk, chunk)
        grads[q].wait()
        hi, lo = split(g[:, cols])
        gh[:, cols], gl[:, cols] = hi, lo
        s1[q] = dot3((ah[0], al[0]), (hi, lo))
        c = remote(s1.at[q], r1.at[q], s1_s.at[q], s1_r.at[q], (e, sibling))
        c.start()
        firsts.append(c)

    def for_chips(q):
        cols = pl.ds(q * chunk, chunk)
        own = dot3((ah[1], al[1]), (gh[:, cols], gl[:, cols]))
        firsts[q].wait_recv()
        total = own + r1[q]
        for c in range(chips):
            s2[q, c] = total[c * rows : (c + 1) * rows]
        for k in range(1, chips):
            c = remote(s2.at[q, near[k]], r2.at[q, k], s2_s.at[q, k], s2_r.at[q, k], at(near[k]))
            c.start()
            seconds[q, k] = c
            sends.append(c)

    def summed(q):
        x = s2[q, chip]
        for k in range(1, chips):
            seconds[q, k].wait_recv()
            x = x + r2[q, k]
        return x

    for_sibling(0)
    for q in range(chunks):
        if q + 1 < chunks:
            for_sibling(q + 1)
        for_chips(q)
    for c in loads[1:]:
        c.wait()
    for b in range(blocks):
        rh[b], rl[b] = split(rt[b])
    lh[...], ll[...] = split(lf[...])

    gathers = {}
    forwards = {}
    squares = jnp.zeros((1, 1), jnp.float32)
    for b in range(blocks):
        parts = [summed(q) for q in range(b * per, (b + 1) * per)]
        x = jnp.concatenate(parts, axis=1)
        cols = pl.ds(b * depth, depth)
        turn = (rh[b], rl[b])
        mean = dot3(split(x), turn) / n
        new_first = 0.9 * fm[:, cols] + 0.1 * mean
        new_second = 0.95 * sm[:, cols] + 0.05 * mean * mean
        normal = new_first / (jnp.sqrt(new_second) + 1e-08)
        turned = dot3(split(normal), turn, NT)
        for j in range(per):
            q = b * per + j
            t[q, d] = turned[:, j * chunk : (j + 1) * chunk]
            for k in near:
                c = remote(t.at[q, d], t.at[q, d], ag_s.at[q, k], ag_r.at[q, k], at(near[k]))
                c.start()
                gathers[q, k] = c
                sends.append(c)
            c = remote(t.at[q, d], t.at[q, d], fw_s.at[q, 0], fw_r.at[q, 0], (e, sibling))
            c.start()
            forwards[q, 0] = c
        fm[:, cols] = new_first
        sm[:, cols] = new_second
        squares = squares + jnp.sum(
            jnp.sum(normal * normal, axis=0, keepdims=True), axis=1, keepdims=True
        )

    outs = [
        pltpu.make_async_copy(fm, first_out, out_sem.at[0]),
        pltpu.make_async_copy(sm, second_out, out_sem.at[1]),
    ]
    for c in outs:
        c.start()
    zs[e] = jnp.broadcast_to(squares, zs.shape[1:])
    tops = []
    for k in range(1, experts):
        c = remote(zs.at[e], zs.at[e], z_s.at[k], z_r.at[k], (lax.rem(e + k, experts), d))
        c.start()
        tops.append(c)

    def arrive(q, k):
        gathers[q, k].wait_recv()
        piece = t.at[q, source[k] * 2 + core]
        c = remote(piece, piece, fw_s.at[q, k], fw_r.at[q, k], (e, sibling))
        c.start()
        forwards[q, k] = c

    for b in range(blocks):
        mine = range(b * per, (b + 1) * per)
        if b == 0:
            for c in tops:
                c.wait_recv()
            ds[d] = jnp.sum(zs[...], axis=0)
            peers = []
            for k in range(1, n):
                c = remote(ds.at[d], ds.at[d], d_s.at[k], d_r.at[k], (e, lax.rem(d + k, n)))
                c.start()
                peers.append(c)
        for q in mine:
            for k in range(1, chips):
                arrive(q, k)
        for q in mine:
            for k in range(chips):
                forwards[q, k].wait_recv()
            cols = pl.ds(q * chunk, chunk)
            acc[:, cols] = dot3((lh[...], ll[...]), split(t[q].reshape(order, chunk)))
            c = pltpu.make_async_copy(acc.at[:, cols], back_out.at[:, cols], b_sem.at[q])
            c.start()
            outs.append(c)

    for c in peers:
        c.wait_recv()
    scale = jnp.sqrt(jnp.sum(ds[...], axis=0) / count + 1e-06)
    sc[...] = jnp.broadcast_to(scale[0:1, 0:1], sc.shape)
    c = pltpu.make_async_copy(sc, scale_out, out_sem.at[2])
    c.start()
    outs.append(c)
    for c in firsts + sends + list(forwards.values()) + tops + peers:
        c.wait_send()
    for c in outs:
        c.wait()


def per_device(gradient, first_moment, second_moment, left_basis, right_basis):
    held, _, order, width = gradient.shape
    blocks, depth = right_basis.shape[1], right_basis.shape[2]
    experts, n = lax.axis_size("expert"), lax.axis_size("dp")
    rows, chips = order // n, n // 2
    chunk = min(256, depth)
    chunks = width // chunk
    half = order // 2
    f32, bf16 = jnp.float32, jnp.bfloat16
    dma = pltpu.SemaphoreType.DMA
    tile = (8, 128)
    scratch = [
        pltpu.VMEM((order, width), f32),
        pltpu.VMEM((order, order), f32),
        pltpu.VMEM((blocks, depth, depth), f32),
        pltpu.VMEM((rows, width), f32),
        pltpu.VMEM((rows, width), f32),
        pltpu.VMEM((n, rows, order), f32),
        pltpu.VMEM((order, width), bf16),
        pltpu.VMEM((order, width), bf16),
        pltpu.VMEM((order, order), bf16),
        pltpu.VMEM((order, order), bf16),
        pltpu.VMEM((2, half, order), bf16),
        pltpu.VMEM((2, half, order), bf16),
        pltpu.VMEM((blocks, depth, depth), bf16),
        pltpu.VMEM((blocks, depth, depth), bf16),
        pltpu.VMEM((chunks, half, chunk), f32),
        pltpu.VMEM((chunks, half, chunk), f32),
        pltpu.VMEM((chunks, chips, rows, chunk), f32),
        pltpu.VMEM((chunks, chips, rows, chunk), f32),
        pltpu.VMEM((chunks, n, rows, chunk), f32),
        pltpu.VMEM((order, width), f32),
        pltpu.VMEM((experts,) + tile, f32),
        pltpu.VMEM((n,) + tile, f32),
        pltpu.VMEM((1, width), f32),
        dma((4,)), dma((chunks,)), dma((3,)), dma((chunks,)),
        dma((chunks,)), dma((chunks,)),
        dma((chunks, chips)), dma((chunks, chips)),
        dma((chunks, chips)), dma((chunks, chips)),
        dma((chunks, chips)), dma((chunks, chips)),
        dma((experts,)), dma((experts,)),
        dma((n,)), dma((n,)),
    ]
    cfg = (experts, n, chunk, held * experts * order * width)
    anywhere = pl.BlockSpec(memory_space=pl.ANY)
    back, scale, new_first, new_second = pl.pallas_call(
        functools.partial(kernel, cfg),
        out_shape=(
            jax.ShapeDtypeStruct((order, width), f32),
            jax.ShapeDtypeStruct((1, width), f32),
            jax.ShapeDtypeStruct((rows, width), f32),
            jax.ShapeDtypeStruct((rows, width), f32),
        ),
        in_specs=[pl.BlockSpec(memory_space=pltpu.HBM)] * 5,
        out_specs=(anywhere,) * 4,
        scratch_shapes=scratch,
        compiler_params=pltpu.CompilerParams(
            collective_id=0, has_side_effects=True, vmem_limit_bytes=56 * 1024 * 1024
        ),
    )(
        gradient.reshape(order, width),
        first_moment.reshape(rows, width),
        second_moment.reshape(rows, width),
        left_basis.reshape(order, order),
        right_basis.reshape(blocks, depth, depth),
    )
    return (back / scale)[None], new_first[None], new_second[None]


def solution(mesh):
    in_specs = (
        P("expert", "dp", None, None),
        P("expert", "dp", None),
        P("expert", "dp", None),
        P("expert", None, None),
        P("expert", None, None, None),
    )
    out_specs = (P("expert", None, None), P("expert", "dp", None), P("expert", "dp", None))
    return jax.shard_map(
        per_device, mesh=mesh, in_specs=in_specs, out_specs=out_specs, check_vma=False
    )
```
